1024 devices in a mesh: blk: 16 (over y_hi, x), dp: 64 (over z, y_lo, core).
Axes of the slice: x: 4, y: 8 (y_hi: 4, y_lo: 2; y = y_hi * 2 + y_lo), z: 16, core: 2. Of those that a mesh axis runs over, the one named last changes fastest.
Arguments:
- image_embeddings: bfloat16 [196608, 640], P(('dp', 'blk')), parts along dimension 0, may hold values from -0.23632812 to 0.23632812
- text_embeddings: bfloat16 [196608, 640], P(('dp', 'blk')), parts along dimension 0, may hold values from -0.23632812 to 0.23632812
- pair_labels: int32 [196608], P(('dp', 'blk')), parts along dimension 0, may hold values from 0 to 3071, as said below
Outputs:
- image_grads: float32 [196608, 640], P(('dp', 'blk')), parts along dimension 0
- text_grads: float32 [196608, 640], P(('dp', 'blk')), parts along dimension 0
The draws below stay inside these ranges and needn't reach their ends.
There are 64 independent parts, one for each index of `dp`. The reference program is written for one: setup_inputs(seed, part) draws one part's arguments, and reference() takes and returns one part's arrays. A program takes and returns all parts, laid end to end along the dimension named above; each array names one. Nothing has to cross between parts.
Inputs may be any that keep to these rules, and one draw needn't show every extreme that they name: pair_labels is a permutation: every text row is paired with exactly one image row.
All inputs are finite; a program needn't handle non-finite values.
Results may differ from the reference program's by a relative error of at most 0.002.
Values may be sent and summed in bfloat16 or wider, within the bound.
No kernel may reach another device: no remote copies, remote signals or barrier semaphores. Data moves between devices by JAX's collectives and lax.ppermute only.
A program may use at most 32 MiB of HBM per device.

```python
import jax
import jax.numpy as jnp

D = 640
TEXTS = 3072
IMAGES = 3072
N_BLK = 16


def draw_pair_labels(key, part):
    key = jax.random.fold_in(key, 7)
    order = jax.random.permutation(key, TEXTS)
    return order.astype(jnp.int32)


def block_levels(stream_key, extent, cuts, smallest, top_value):
    level = 1.0
    for dim, blocks in cuts:
        steps = jax.random.uniform(jax.random.fold_in(jax.random.fold_in(stream_key, 6), dim), (blocks,), jnp.float32, smallest / len(cuts), top_value / len(cuts))
        level = level * jnp.repeat(jnp.exp(steps), extent[dim] // blocks).reshape((-1,) + (1,) * (len(extent) - 1 - dim))
    return level


def normal_values(stream_key, extent, spread, bound, cuts=(), kind=jnp.bfloat16):
    drawn = spread * jax.random.normal(stream_key, extent, jnp.float32)
    if cuts:
        drawn = drawn * block_levels(stream_key, extent, cuts, -0.22, 0.18)
    return jnp.clip(drawn, -bound, bound).astype(kind)


def setup_inputs(seed: int = 0, part: int = 0) -> dict:
    arg_keys = jax.random.split(jax.random.key(seed), 4)
    own_keys = jax.random.split(jax.random.fold_in(arg_keys[3], part), 4)
    return {
        "image_embeddings": normal_values(own_keys[0], (IMAGES, D), (1.0 / D ** 0.5), 0.23632812, ((0, 16),)),
        "text_embeddings": normal_values(own_keys[1], (TEXTS, D), (1.0 / D ** 0.5), 0.23632812, ((0, 16),)),
        "pair_labels": draw_pair_labels(jax.random.fold_in(jax.random.fold_in(arg_keys[3], part), 71), part),
    }


logit_scale = 25.0
logit_bias = -1.0


def reference(image_embeddings, text_embeddings, pair_labels):
    logits = logit_scale * jnp.dot(image_embeddings, text_embeddings.T, preferred_element_type=jnp.float32) + logit_bias
    columns = jnp.arange(TEXTS, dtype=jnp.int32)[None, :]
    signs = jnp.where(pair_labels[:, None] == columns, jnp.float32(1.0), jnp.float32(-1.0))
    coeff = (-signs * jax.nn.sigmoid(-signs * logits) / N_BLK).astype(jnp.bfloat16)
    image_grads = logit_scale * jnp.dot(coeff, text_embeddings, preferred_element_type=jnp.float32)
    text_grads = logit_scale * jnp.dot(coeff.T, image_embeddings, preferred_element_type=jnp.float32)
    return image_grads, text_grads
```

```python
import functools

import jax
import jax.numpy as jnp
from jax import lax
from jax.experimental import pallas as pl
from jax.experimental.pallas import tpu as pltpu
from jax.sharding import Mesh, PartitionSpec as P

logit_scale = 25.0
logit_bias = -1.0
sides = 4
send_type = jnp.bfloat16
label_base = 64
pad_rows = 16

nt = (((1,), (1,)), ((), ()))
tn = (((0,), (0,)), ((), ()))


def shifted(value, axis, steps):
    pairs = [(source, (source + steps) % sides) for source in range(sides)]
    return lax.ppermute(value, axis, pairs)


def coefficients(text_rows, images, labels, text_ids):
    logits = (
        logit_scale
        * lax.dot_general(text_rows, images, nt, preferred_element_type=jnp.float32)
        + logit_bias
    )
    paired = labels == text_ids
    small = 1.0 / (1.0 + jnp.exp(jnp.where(paired, logits, -logits)))
    return jnp.where(paired, -small, small).astype(jnp.bfloat16)


def fill_images(bundles, images, labels):
    rows = bundles[0].shape[0] - pad_rows
    for k, bundle in enumerate(bundles):
        images[k * rows : (k + 1) * rows, :] = bundle[:rows, :]
        digits = bundle[rows:, :].astype(jnp.float32)
        labels[0:1, k * 256 : k * 256 + rows] = label_base * digits[0:1, :rows] + digits[1:2, :rows]


def near_kernel(scale, position, i0, i1, i2, i3, t0, t1, t2, own, up, down, image_part, labels_out, images_out, labs, coeff):
    rows = t0.shape[0]
    bundles = (i0, i1, i2, i3)
    for k, bundle in enumerate(bundles):
        images_out[k * rows : (k + 1) * rows, :] = bundle[:rows, :]
        digits = bundle[rows:, :].astype(jnp.float32)
        labs[k : k + 1, :] = label_base * digits[0:1, :rows] + digits[1:2, :rows]
    labels_out[...] = jnp.concatenate([labs[k : k + 1, :] for k in range(sides)], axis=1)
    total = None
    for n, (texts, out) in enumerate(((t0, own), (t1, up), (t2, down))):
        ids = position[n].astype(jnp.float32) + lax.broadcasted_iota(jnp.int32, (rows, 1), 0).astype(jnp.float32)
        c = coefficients(texts[...], images_out[...], labels_out[...], ids)
        coeff[n * rows : (n + 1) * rows, :] = c
        out[...] = (scale * jnp.dot(c, images_out[...], preferred_element_type=jnp.float32)).astype(out.dtype)
    total = None
    for n, texts in enumerate((t0, t1, t2)):
        term = lax.dot_general(coeff[n * rows : (n + 1) * rows, :], texts[...], tn, preferred_element_type=jnp.float32)
        total = term if total is None else total + term
    image_part[...] = total


def far_kernel(scale, position, texts, images, labels, image_part, far, g0, g1, g2, g3):
    rows = texts.shape[0]
    ids = position[3].astype(jnp.float32) + lax.broadcasted_iota(jnp.int32, (rows, 1), 0).astype(jnp.float32)
    c = coefficients(texts[...], images[...], labels[...], ids)
    total = scale * (image_part[...] + lax.dot_general(c, texts[...], tn, preferred_element_type=jnp.float32))
    far[...] = (scale * jnp.dot(c, images[...], preferred_element_type=jnp.float32)).astype(far.dtype)
    for k, out in enumerate((g0, g1, g2, g3)):
        out[...] = total[k * rows : (k + 1) * rows, :].astype(out.dtype)


vmem = pl.BlockSpec(memory_space=pltpu.VMEM)
smem = pl.BlockSpec(memory_space=pltpu.SMEM)
params = pltpu.CompilerParams(vmem_limit_bytes=48 * 1024 * 1024)


def on_device(image_embeddings, text_embeddings, pair_labels):
    rows, width = text_embeddings.shape
    y, x = lax.axis_index("yh"), lax.axis_index("xx")
    scale = logit_scale / (sides * sides)

    high, low = pair_labels // label_base, pair_labels % label_base
    digits = jnp.zeros((pad_rows, width), jnp.bfloat16)
    digits = digits.at[0, :rows].set(high.astype(jnp.bfloat16)).at[1, :rows].set(low.astype(jnp.bfloat16))
    bundle = jnp.concatenate([image_embeddings, digits], axis=0)

    text_up = shifted(text_embeddings, "yh", 1)
    text_down = shifted(text_embeddings, "yh", -1)
    image_1 = shifted(bundle, "xx", 1)
    image_3 = shifted(bundle, "xx", -1)
    image_2 = shifted(bundle, "xx", 2)
    text_far = shifted(text_embeddings, "yh", 2)

    owners = (y + jnp.array([0, sides - 1, 1, 2], jnp.int32)) % sides
    position = (owners * sides + x) * rows

    f32 = jnp.float32
    block = (rows, width)
    own, up, down, part, labels, images = pl.pallas_call(
        functools.partial(near_kernel, scale),
        out_shape=[
            jax.ShapeDtypeStruct(block, f32),
            jax.ShapeDtypeStruct(block, send_type),
            jax.ShapeDtypeStruct(block, send_type),
            jax.ShapeDtypeStruct((sides * rows, width), f32),
            jax.ShapeDtypeStruct((1, sides * rows), f32),
            jax.ShapeDtypeStruct((sides * rows, width), jnp.bfloat16),
        ],
        in_specs=[smem] + [vmem] * 7,
        out_specs=[vmem] * 6,
        scratch_shapes=[pltpu.VMEM((8, rows), f32), pltpu.VMEM((3 * rows, sides * rows), jnp.bfloat16)],
        compiler_params=params,
        cost_estimate=pl.CostEstimate(flops=6 * 3 * sides * rows * rows * width, bytes_accessed=6 << 20, transcendentals=0),
    )(position, bundle, image_1, image_2, image_3, text_embeddings, text_up, text_down)
    back_up = shifted(up, "yh", -1)
    back_down = shifted(down, "yh", 1)

    far, g0, g1, g2, g3 = pl.pallas_call(
        functools.partial(far_kernel, scale),
        out_shape=[jax.ShapeDtypeStruct(block, send_type), jax.ShapeDtypeStruct(block, f32)]
        + [jax.ShapeDtypeStruct(block, send_type)] * 3,
        in_specs=[smem] + [vmem] * 4,
        out_specs=[vmem] * 5,
        compiler_params=params,
        cost_estimate=pl.CostEstimate(flops=6 * sides * rows * rows * width, bytes_accessed=6 << 20, transcendentals=0),
    )(position, text_far, images, labels, part)
    back_far = shifted(far, "yh", 2)
    grad_1 = shifted(g1, "xx", -1)
    grad_3 = shifted(g3, "xx", 1)
    grad_2 = shifted(g2, "xx", 2)

    text_grads = own + back_up.astype(f32) + back_down.astype(f32) + back_far.astype(f32)
    image_grads = g0 + grad_1.astype(f32) + grad_3.astype(f32) + grad_2.astype(f32)
    return image_grads, text_grads


def solution(mesh):
    grid = Mesh(mesh.devices.reshape(sides, sides, -1), ("yh", "xx", "dp"))
    rows = P(("dp", "yh", "xx"), None)
    return jax.shard_map(
        on_device,
        mesh=grid,
        in_specs=(rows, rows, P(("dp", "yh", "xx"))),
        out_specs=(rows, rows),
        check_vma=False,
    )
```

```python
import functools

import jax
import jax.numpy as jnp
from jax import lax
from jax.experimental import pallas as pl
from jax.experimental.pallas import tpu as pltpu
from jax.sharding import Mesh, PartitionSpec as P

logit_scale = 25.0
logit_bias = -1.0
sides = 4
send_type = jnp.bfloat16
label_base = 64
pad_rows = 16

nt = (((1,), (1,)), ((), ()))
tn = (((0,), (0,)), ((), ()))
vmem = pl.BlockSpec(memory_space=pltpu.VMEM)
params = pltpu.CompilerParams(vmem_limit_bytes=48 * 1024 * 1024)


def shifted(value, axis, steps):
    pairs = [(source, (source + steps) % sides) for source in range(sides)]
    return lax.ppermute(value, axis, pairs)


def together(*values):
    return lax.optimization_barrier(values)


def bundle_kernel(images, labels, out):
    rows, width = images.shape
    out[:rows, :] = images[...]
    value = labels[...]
    high = value // label_base
    low = value - high * label_base
    line = lax.broadcasted_iota(jnp.int32, (pad_rows, rows), 0)
    digits = jnp.where(line == 0, high, jnp.where(line == 1, low, 0))
    out[rows:, :rows] = digits.astype(jnp.float32).astype(jnp.bfloat16)
    out[rows:, rows:] = jnp.zeros((pad_rows, width - rows), jnp.bfloat16)


def coefficients(text_rows, images, labels, text_ids):
    logits = (
        logit_scale
        * lax.dot_general(text_rows, images, nt, preferred_element_type=jnp.float32)
        + logit_bias
    )
    paired = labels == text_ids
    small = 1.0 / (1.0 + jnp.exp(jnp.where(paired, logits, -logits)))
    return jnp.where(paired, -small, small).astype(jnp.bfloat16)


def text_kernel(scale, bundles, t0, t2, t1, t3, own, up, far, down, images, coeff, labs):
    rows = t0.shape[0]
    for k in range(sides):
        images[k * rows : (k + 1) * rows, :] = bundles[k, :rows, :]
        digits = bundles[k, rows:, :].astype(jnp.float32)
        labs[k : k + 1, :] = label_base * digits[0:1, :rows] + digits[1:2, :rows]
    labels = jnp.concatenate([labs[k : k + 1, :] for k in range(sides)], axis=1)
    y, x = lax.axis_index("yh"), lax.axis_index("xx")
    line = lax.broadcasted_iota(jnp.int32, (rows, 1), 0)
    for n, (texts, out) in enumerate(((t0, own), (t1, up), (t2, far), (t3, down))):
        first = (lax.rem(y + (sides - n), sides) * sides + x) * rows
        ids = (first + line).astype(jnp.float32)
        c = coefficients(texts[...], images[...], labels, ids)
        coeff[n * rows : (n + 1) * rows, :] = c
        out[...] = (scale * jnp.dot(c, images[...], preferred_element_type=jnp.float32)).astype(out.dtype)


def image_kernel(scale, coeff, t0, t1, t2, t3, g0, g1, g2, g3, total):
    rows = t0.shape[0]
    value = None
    for n, texts in enumerate((t0, t1, t2, t3)):
        term = lax.dot_general(coeff[n * rows : (n + 1) * rows, :], texts[...], tn, preferred_element_type=jnp.float32)
        value = term if value is None else value + term
    for k in range(sides):
        total[k] = scale * value[k * rows : (k + 1) * rows, :]
    x = lax.axis_index("xx")
    for k, out in enumerate((g0, g1, g2, g3)):
        out[...] = total[lax.rem(x + (sides - k), sides)].astype(out.dtype)


def sum_kernel(h0, y1, y2, y3, g0, x1, x2, x3, image_grads, text_grads):
    f32 = jnp.float32
    image_grads[...] = g0[...] + x1[...].astype(f32) + x2[...].astype(f32) + x3[...].astype(f32)
    text_grads[...] = h0[...] + y1[...].astype(f32) + y2[...].astype(f32) + y3[...].astype(f32)


def call(kernel, inputs, shapes, scratch=(), flops=0):
    return pl.pallas_call(
        kernel,
        out_shape=shapes,
        in_specs=[vmem] * inputs,
        out_specs=[vmem] * len(shapes),
        scratch_shapes=list(scratch),
        compiler_params=params,
        cost_estimate=pl.CostEstimate(flops=flops, bytes_accessed=4 << 20, transcendentals=0),
    )


def on_device(image_embeddings, text_embeddings, pair_labels):
    rows, width = text_embeddings.shape
    scale = logit_scale / (sides * sides)
    f32 = jnp.float32
    block = (rows, width)
    every = sides * rows

    (bundle,) = call(bundle_kernel, 2, [jax.ShapeDtypeStruct((rows + pad_rows, width), jnp.bfloat16)])(
        image_embeddings, pair_labels.reshape(1, rows)
    )
    texts = text_embeddings
    text_2 = shifted(texts, "yh", 2)
    text_3 = shifted(texts, "yh", -1)
    text_1 = shifted(texts, "yh", 1)
    bundles = lax.all_gather(bundle, "xx", axis=0)

    own, up, far, down, images, coeff = call(
        functools.partial(text_kernel, scale),
        5,
        [
            jax.ShapeDtypeStruct(block, f32),
            jax.ShapeDtypeStruct(block, send_type),
            jax.ShapeDtypeStruct(block, send_type),
            jax.ShapeDtypeStruct(block, send_type),
            jax.ShapeDtypeStruct((every, width), jnp.bfloat16),
            jax.ShapeDtypeStruct((every, every), jnp.bfloat16),
        ],
        [pltpu.VMEM((8, rows), f32)],
        4 * every * every * width,
    )(bundles, texts, text_2, text_1, text_3)
    back_2 = shifted(far, "yh", 2)
    back_1 = shifted(up, "yh", -1)
    back_3 = shifted(down, "yh", 1)
    g0, g1, g2, g3 = call(
        functools.partial(image_kernel, scale),
        5,
        [jax.ShapeDtypeStruct(block, f32)] + [jax.ShapeDtypeStruct(block, send_type)] * 3,
        [pltpu.VMEM((sides,) + block, f32)],
        2 * every * every * width,
    )(coeff, texts, text_1, text_2, text_3)
    grad_1 = shifted(g1, "xx", -1)
    grad_2 = shifted(g2, "xx", 2)
    grad_3 = shifted(g3, "xx", 1)
    image_grads, text_grads = call(sum_kernel, 8, [jax.ShapeDtypeStruct(block, f32)] * 2)(
        own, back_2, back_1, back_3, g0, grad_2, grad_1, grad_3
    )
    return image_grads, text_grads


def solution(mesh):
    grid = Mesh(mesh.devices.reshape(sides, sides, -1), ("yh", "xx", "dp"))
    rows = P(("dp", "yh", "xx"), None)
    return jax.shard_map(
        on_device,
        mesh=grid,
        in_specs=(rows, rows, P(("dp", "yh", "xx"))),
        out_specs=(rows, rows),
        check_vma=False,
    )
```

```python
import functools

import jax
import jax.numpy as jnp
from jax import lax
from jax.experimental import pallas as pl
from jax.experimental.pallas import tpu as pltpu
from jax.sharding import Mesh, PartitionSpec as P

logit_scale = 25.0
logit_bias = -1.0
sides = 4
send_type = jnp.bfloat16
label_base = 64
pad_rows = 16

nt = (((1,), (1,)), ((), ()))
tn = (((0,), (0,)), ((), ()))
vmem = pl.BlockSpec(memory_space=pltpu.VMEM)
hbm = pl.BlockSpec(memory_space=pltpu.HBM)
params = pltpu.CompilerParams(vmem_limit_bytes=48 * 1024 * 1024)


def shifted(value, axis, steps):
    pairs = [(source, (source + steps) % sides) for source in range(sides)]
    return lax.ppermute(value, axis, pairs)


def together(*values):
    return lax.optimization_barrier(values)


def copies_kernel(texts, out, sems):
    moves = [pltpu.make_async_copy(texts, out.at[k], sems.at[k]) for k in range(sides)]
    for move in moves:
        move.start()
    for move in moves:
        move.wait()


def bundle_kernel(images, labels, out):
    rows, width = images.shape
    out[:rows, :] = images[...]
    value = labels[...]
    high = value // label_base
    low = value - high * label_base
    line = lax.broadcasted_iota(jnp.int32, (pad_rows, rows), 0)
    digits = jnp.where(line == 0, high, jnp.where(line == 1, low, 0))
    out[rows:, :rows] = digits.astype(jnp.float32).astype(jnp.bfloat16)
    out[rows:, rows:] = jnp.zeros((pad_rows, width - rows), jnp.bfloat16)


def coefficients(text_rows, images, labels, text_ids):
    logits = (
        logit_scale
        * lax.dot_general(text_rows, images, nt, preferred_element_type=jnp.float32)
        + logit_bias
    )
    paired = labels == text_ids
    small = 1.0 / (1.0 + jnp.exp(jnp.where(paired, logits, -logits)))
    return jnp.where(paired, -small, small).astype(jnp.bfloat16)


def text_ids(first, rows):
    line = lax.broadcasted_iota(jnp.int32, (rows, 1), 0)
    return (first * rows + line).astype(jnp.float32)


def near_kernel(scale, i0, i1, i2, i3, texts, own, images, labels, coeff, labs):
    rows = own.shape[0]
    for k, bundle in enumerate((i0, i1, i2, i3)):
        images[k * rows : (k + 1) * rows, :] = bundle[:rows, :]
        digits = bundle[rows:, :].astype(jnp.float32)
        labs[k : k + 1, :] = label_base * digits[0:1, :rows] + digits[1:2, :rows]
    labels[...] = jnp.concatenate([labs[k : k + 1, :] for k in range(sides)], axis=1)
    y, x = lax.axis_index("yh"), lax.axis_index("xx")
    c = coefficients(texts[...], images[...], labels[...], text_ids(y * sides + x, rows))
    coeff[...] = c
    own[...] = scale * jnp.dot(c, images[...], preferred_element_type=jnp.float32)


def far_kernel(scale, stack, images, labels, parts, coeff, made, sems):
    rows = stack.shape[1]
    y, x = lax.axis_index("yh"), lax.axis_index("xx")
    moves = []
    for n in range(sides - 1):
        owner = lax.rem(y + (n + 1), sides)
        c = coefficients(stack[owner], images[...], labels[...], text_ids(owner * sides + x, rows))
        coeff[n * rows : (n + 1) * rows, :] = c
        made[n] = (scale * jnp.dot(c, images[...], preferred_element_type=jnp.float32)).astype(made.dtype)
        moves.append(pltpu.make_async_copy(made.at[n], parts.at[owner], sems.at[n]))
        moves[-1].start()
    for move in moves:
        move.wait()


def image_kernel(scale, near, coeff, texts, stack, g0, g1, g2, g3):
    rows = g0.shape[0]
    y = lax.axis_index("yh")
    value = lax.dot_general(near[...], texts[...], tn, preferred_element_type=jnp.float32)
    for n in range(sides - 1):
        value = value + lax.dot_general(
            coeff[n * rows : (n + 1) * rows, :],
            stack[lax.rem(y + (n + 1), sides)],
            tn,
            preferred_element_type=jnp.float32,
        )
    for k, out in enumerate((g0, g1, g2, g3)):
        out[...] = (scale * value[k * rows : (k + 1) * rows, :]).astype(out.dtype)


def sum_kernel(own, parts, g0, x1, x2, x3, image_grads, text_grads):
    f32 = jnp.float32
    image_grads[...] = g0[...] + x1[...].astype(f32) + x2[...].astype(f32) + x3[...].astype(f32)
    y = lax.axis_index("yh")
    total = own[...]
    for step in range(1, sides):
        total = total + parts[lax.rem(y + step, sides)].astype(f32)
    text_grads[...] = total


def call(kernel, shapes, scratch=(), flops=0, outputs=None):
    def run(*operands):
        return pl.pallas_call(
            kernel,
            out_shape=shapes,
            in_specs=[vmem] * len(operands),
            out_specs=[vmem] * len(shapes) if outputs is None else outputs,
            scratch_shapes=list(scratch),
            compiler_params=params,
            cost_estimate=pl.CostEstimate(flops=flops, bytes_accessed=4 << 20, transcendentals=0),
        )(*operands)

    return run


def on_device(image_embeddings, text_embeddings, pair_labels):
    rows, width = text_embeddings.shape
    scale = logit_scale / (sides * sides)
    f32 = jnp.float32
    block = (rows, width)
    every = sides * rows

    dots = 2 * rows * every * width
    half = jnp.bfloat16
    shape = jax.ShapeDtypeStruct

    (copies,) = call(
        copies_kernel,
        [shape((sides,) + block, half)],
        [pltpu.SemaphoreType.DMA((sides,))],
        outputs=[hbm],
    )(text_embeddings)
    (bundle,) = call(bundle_kernel, [shape((rows + pad_rows, width), half)])(
        image_embeddings, pair_labels.reshape(1, rows)
    )
    stack = lax.all_to_all(copies, "yh", 0, 0)
    image_1 = shifted(bundle, "xx", 1)
    image_2 = shifted(bundle, "xx", 2)
    image_3 = shifted(bundle, "xx", -1)

    own, images, labels, near = call(
        functools.partial(near_kernel, scale),
        [shape(block, f32), shape((every, width), half), shape((1, every), f32), shape((rows, every), half)],
        [pltpu.VMEM((8, rows), f32)],
        2 * dots,
    )(bundle, image_1, image_2, image_3, text_embeddings)
    parts, coeff = call(
        functools.partial(far_kernel, scale),
        [shape((sides,) + block, send_type), shape(((sides - 1) * rows, every), half)],
        [pltpu.VMEM((sides - 1,) + block, send_type), pltpu.SemaphoreType.DMA((sides - 1,))],
        6 * dots,
        outputs=[hbm, vmem],
    )(stack, images, labels)
    parts = lax.all_to_all(parts, "yh", 0, 0)
    g0, g1, g2, g3 = call(
        functools.partial(image_kernel, scale),
        [shape(block, f32)] + [shape(block, send_type)] * 3,
        (),
        4 * dots,
    )(near, coeff, text_embeddings, stack)
    grad_1 = shifted(g1, "xx", -1)
    grad_2 = shifted(g2, "xx", 2)
    grad_3 = shifted(g3, "xx", 1)
    image_grads, text_grads = call(sum_kernel, [shape(block, f32)] * 2)(
        own, parts, g0, grad_1, grad_2, grad_3
    )
    return image_grads, text_grads


def solution(mesh):
    grid = Mesh(mesh.devices.reshape(sides, sides, -1), ("yh", "xx", "dp"))
    rows = P(("dp", "yh", "xx"), None)
    return jax.shard_map(
        on_device,
        mesh=grid,
        in_specs=(rows, rows, P(("dp", "yh", "xx"))),
        out_specs=(rows, rows),
        check_vma=False,
    )
```

```python
import functools

import jax
import jax.numpy as jnp
from jax import lax
from jax.experimental import pallas as pl
from jax.experimental.pallas import tpu as pltpu
from jax.sharding import Mesh, PartitionSpec as P

logit_scale = 25.0
logit_bias = -1.0
sides = 4
send_type = jnp.bfloat16
label_base = 64
log2_e = 1.4426950408889634
pad_rows = 16
chunks = 4

nt = (((1,), (1,)), ((), ()))
tn = (((0,), (0,)), ((), ()))
vmem = pl.BlockSpec(memory_space=pltpu.VMEM)
hbm = pl.BlockSpec(memory_space=pltpu.HBM)


def shifted(value, axis, steps):
    pairs = [(source, (source + steps) % sides) for source in range(sides)]
    return lax.ppermute(value, axis, pairs)


def together(*values):
    return lax.optimization_barrier(values)


def copies_kernel(texts, out, held, in_sems, out_sems):
    part = texts.shape[0] // chunks
    spans = [pl.ds(c * part, part) for c in range(chunks)]
    reads = [pltpu.make_async_copy(texts.at[span], held.at[span], in_sems.at[c]) for c, span in enumerate(spans)]
    for read in reads:
        read.start()
    writes = []
    for c, span in enumerate(spans):
        reads[c].wait()
        for k in range(sides):
            writes.append(pltpu.make_async_copy(held.at[span], out.at[k, span], out_sems.at[c, k]))
            writes[-1].start()
    for write in writes:
        write.wait()


def bundle_kernel(images, labels, out):
    rows, width = images.shape
    out[:rows, :] = images[...]
    value = labels[...]
    high = value // label_base
    low = value - high * label_base
    line = lax.broadcasted_iota(jnp.int32, (pad_rows, rows), 0)
    digits = jnp.where(line == 0, high, jnp.where(line == 1, low, 0))
    out[rows:, :rows] = digits.astype(jnp.float32).astype(jnp.bfloat16)
    out[rows:, rows:] = jnp.zeros((pad_rows, width - rows), jnp.bfloat16)


def coefficients(text_rows, images, labels, ids):
    dots = lax.dot_general(text_rows, images, nt, preferred_element_type=jnp.float32)
    sign = jnp.where(labels == ids, jnp.float32(-1.0), jnp.float32(1.0))
    power = (dots * (-logit_scale * log2_e) - logit_bias * log2_e) * sign
    return (sign * (1.0 / (1.0 + jnp.exp2(power)))).astype(jnp.bfloat16)


def text_ids(first, rows):
    line = lax.broadcasted_iota(jnp.int32, (rows, 1), 0)
    return (first * rows + line).astype(jnp.float32)


def near_kernel(scale, i0, i1, i2, i3, texts, own, images, labels, labs):
    rows = own.shape[0]
    for k, bundle in enumerate((i0, i1, i2, i3)):
        images[k * rows : (k + 1) * rows, :] = bundle[:rows, :]
        digits = bundle[rows:, :].astype(jnp.float32)
        labs[k : k + 1, :] = label_base * digits[0:1, :rows] + digits[1:2, :rows]
    labels[...] = jnp.concatenate([labs[k : k + 1, :] for k in range(sides)], axis=1)
    y, x = lax.axis_index("yh"), lax.axis_index("xx")
    c = coefficients(texts[...], images[...], labels[...], text_ids(y * sides + x, rows))
    own[...] = scale * jnp.dot(c, images[...], preferred_element_type=jnp.float32)


def far_kernel(scale, stack, images, labels, parts, texts, made, sems):
    rows = stack.shape[1]
    y, x = lax.axis_index("yh"), lax.axis_index("xx")
    owners = [lax.rem(y + n, sides) for n in range(1, sides)]
    for n, owner in enumerate(owners):
        texts[n * rows : (n + 1) * rows, :] = stack[owner]
    ids = jnp.concatenate([text_ids(owner * sides + x, rows) for owner in owners], axis=0)
    coeff = coefficients(texts[...], images[...], labels[...], ids)
    moves = []
    part = scale * jnp.dot(coeff, images[...], preferred_element_type=jnp.float32)
    for n, owner in enumerate(owners):
        made[n] = part[n * rows : (n + 1) * rows, :].astype(made.dtype)
        moves.append(pltpu.make_async_copy(made.at[n], parts.at[owner], sems.at[n]))
        moves[-1].start()
    for move in moves:
        move.wait()


def image_kernel(scale, images, labels, stack, g0, g1, g2, g3):
    rows = g0.shape[0]
    y, x = lax.axis_index("yh"), lax.axis_index("xx")
    value = None
    for n in range(sides):
        owner = lax.rem(y + n, sides)
        c = coefficients(stack[owner], images[...], labels[...], text_ids(owner * sides + x, rows))
        term = lax.dot_general(c, stack[owner], tn, preferred_element_type=jnp.float32)
        value = term if value is None else value + term
    for k, out in enumerate((g0, g1, g2, g3)):
        out[...] = (scale * value[k * rows : (k + 1) * rows, :]).astype(out.dtype)


def image_sum_kernel(g0, x1, x2, x3, image_grads):
    f32 = jnp.float32
    image_grads[...] = g0[...] + x1[...].astype(f32) + x2[...].astype(f32) + x3[...].astype(f32)


def text_sum_kernel(own, parts, text_grads):
    y = lax.axis_index("yh")
    total = own[...]
    for step in range(1, sides):
        total = total + parts[lax.rem(y + step, sides)].astype(jnp.float32)
    text_grads[...] = total


def call(kernel, shapes, scratch=(), flops=0, inputs=vmem, outputs=None, grant=48):
    def run(*operands):
        return pl.pallas_call(
            kernel,
            out_shape=shapes,
            in_specs=[inputs] * len(operands),
            out_specs=[vmem] * len(shapes) if outputs is None else outputs,
            scratch_shapes=list(scratch),
            compiler_params=pltpu.CompilerParams(vmem_limit_bytes=grant * 1024 * 1024),
            cost_estimate=pl.CostEstimate(flops=flops, bytes_accessed=4 << 20, transcendentals=0),
        )(*operands)

    return run


def on_device(image_embeddings, text_embeddings, pair_labels):
    rows, width = text_embeddings.shape
    scale = logit_scale / (sides * sides)
    f32 = jnp.float32
    block = (rows, width)
    every = sides * rows

    dots = 2 * rows * every * width
    half = jnp.bfloat16
    shape = jax.ShapeDtypeStruct

    (copies,) = call(
        copies_kernel,
        [shape((sides,) + block, half)],
        [pltpu.VMEM(block, half), pltpu.SemaphoreType.DMA((chunks,)), pltpu.SemaphoreType.DMA((chunks, sides))],
        inputs=hbm,
        outputs=[hbm],
        grant=60,
    )(text_embeddings)
    (bundle,) = call(bundle_kernel, [shape((rows + pad_rows, width), half)])(
        image_embeddings, pair_labels.reshape(1, rows)
    )
    stack = lax.all_to_all(copies, "yh", 0, 0)
    image_1 = shifted(bundle, "xx", 1)
    image_2 = shifted(bundle, "xx", 2)
    image_3 = shifted(bundle, "xx", -1)

    own, images, labels = call(
        functools.partial(near_kernel, scale),
        [shape(block, f32), shape((every, width), half), shape((1, every), f32)],
        [pltpu.VMEM((8, rows), f32)],
        2 * dots,
    )(bundle, image_1, image_2, image_3, text_embeddings)
    (parts,) = call(
        functools.partial(far_kernel, scale),
        [shape((sides,) + block, send_type)],
        [pltpu.VMEM(((sides - 1) * rows, width), half), pltpu.VMEM((sides - 1,) + block, send_type), pltpu.SemaphoreType.DMA((sides - 1,))],
        6 * dots,
        outputs=[hbm],
    )(stack, images, labels)
    parts = lax.all_to_all(parts, "yh", 0, 0)
    g0, g1, g2, g3 = call(
        functools.partial(image_kernel, scale),
        [shape(block, f32)] + [shape(block, send_type)] * 3,
        (),
        4 * dots,
    )(images, labels, stack)
    grad_1 = shifted(g1, "xx", -1)
    grad_2 = shifted(g2, "xx", 2)
    grad_3 = shifted(g3, "xx", 1)
    (image_grads,) = call(image_sum_kernel, [shape(block, f32)])(g0, grad_1, grad_2, grad_3)
    (text_grads,) = call(text_sum_kernel, [shape(block, f32)])(own, parts)
    return image_grads, text_grads


def solution(mesh):
    grid = Mesh(mesh.devices.reshape(sides, sides, -1), ("yh", "xx", "dp"))
    rows = P(("dp", "yh", "xx"), None)
    return jax.shard_map(
        on_device,
        mesh=grid,
        in_specs=(rows, rows, P(("dp", "yh", "xx"))),
        out_specs=(rows, rows),
        check_vma=False,
    )
```

```python
import functools

import jax
import jax.numpy as jnp
from jax import lax
from jax.experimental import pallas as pl
from jax.experimental.pallas import tpu as pltpu
from jax.sharding import Mesh, PartitionSpec as P

logit_scale = 25.0
logit_bias = -1.0
sides = 4
send_type = jnp.bfloat16
label_base = 64
log2_e = 1.4426950408889634
pad_rows = 16
chunks = 4

nt = (((1,), (1,)), ((), ()))
tn = (((0,), (0,)), ((), ()))
vmem = pl.BlockSpec(memory_space=pltpu.VMEM)
hbm = pl.BlockSpec(memory_space=pltpu.HBM)


def shifted(value, axis, steps):
    pairs = [(source, (source + steps) % sides) for source in range(sides)]
    return lax.ppermute(value, axis, pairs)


def together(*values):
    return lax.optimization_barrier(values)


def copies_kernel(texts, out, held, in_sems, out_sems):
    part = texts.shape[0] // chunks
    spans = [pl.ds(c * part, part) for c in range(chunks)]
    reads = [pltpu.make_async_copy(texts.at[span], held.at[span], in_sems.at[c]) for c, span in enumerate(spans)]
    for read in reads:
        read.start()
    writes = []
    for c, span in enumerate(spans):
        reads[c].wait()
        for k in range(sides):
            writes.append(pltpu.make_async_copy(held.at[span], out.at[k, span], out_sems.at[c, k]))
            writes[-1].start()
    for write in writes:
        write.wait()


def bundle_kernel(images, labels, out):
    rows, width = images.shape
    out[:rows, :] = images[...]
    value = labels[...]
    high = value // label_base
    low = value - high * label_base
    line = lax.broadcasted_iota(jnp.int32, (pad_rows, rows), 0)
    digits = jnp.where(line == 0, high, jnp.where(line == 1, low, 0))
    out[rows:, :rows] = digits.astype(jnp.float32).astype(jnp.bfloat16)
    out[rows:, rows:] = jnp.zeros((pad_rows, width - rows), jnp.bfloat16)


def coefficients(text_rows, images, labels, ids):
    dots = lax.dot_general(text_rows, images, nt, preferred_element_type=jnp.float32)
    sign = jnp.where(labels == ids, jnp.float32(-1.0), jnp.float32(1.0))
    power = (dots * (-logit_scale * log2_e) - logit_bias * log2_e) * sign
    return (sign * (1.0 / (1.0 + jnp.exp2(power)))).astype(jnp.bfloat16)


def text_ids(first, rows):
    line = lax.broadcasted_iota(jnp.int32, (rows, 1), 0)
    return (first * rows + line).astype(jnp.float32)


def near_kernel(scale, i0, i1, i2, i3, texts, own, images, labels, labs):
    rows = own.shape[0]
    for k, bundle in enumerate((i0, i1, i2, i3)):
        images[k * rows : (k + 1) * rows, :] = bundle[:rows, :]
        digits = bundle[rows:, :].astype(jnp.float32)
        labs[k : k + 1, :] = label_base * digits[0:1, :rows] + digits[1:2, :rows]
    labels[...] = jnp.concatenate([labs[k : k + 1, :] for k in range(sides)], axis=1)
    y, x = lax.axis_index("yh"), lax.axis_index("xx")
    c = coefficients(texts[...], images[...], labels[...], text_ids(y * sides + x, rows))
    own[...] = scale * jnp.dot(c, images[...], preferred_element_type=jnp.float32)


def far_kernel(scale, stack, images, labels, parts, texts, made, sems):
    rows = stack.shape[1]
    y, x = lax.axis_index("yh"), lax.axis_index("xx")
    owners = [lax.rem(y + n, sides) for n in range(1, sides)]
    for n, owner in enumerate(owners):
        texts[n * rows : (n + 1) * rows, :] = stack[owner]
    ids = jnp.concatenate([text_ids(owner * sides + x, rows) for owner in owners], axis=0)
    coeff = coefficients(texts[...], images[...], labels[...], ids)
    moves = []
    part = scale * jnp.dot(coeff, images[...], preferred_element_type=jnp.float32)
    for n, owner in enumerate(owners):
        made[n] = part[n * rows : (n + 1) * rows, :].astype(made.dtype)
        moves.append(pltpu.make_async_copy(made.at[n], parts.at[owner], sems.at[n]))
        moves[-1].start()
    for move in moves:
        move.wait()


def image_kernel(scale, images, labels, stack, g0, g1, g2, g3):
    rows = g0.shape[0]
    x = lax.axis_index("xx")
    ids = jnp.concatenate([text_ids(n * sides + x, rows) for n in range(sides)], axis=0)
    texts = stack[...].reshape(sides * rows, stack.shape[2])
    c = coefficients(texts, images[...], labels[...], ids)
    value = scale * lax.dot_general(c, texts, tn, preferred_element_type=jnp.float32)
    for k, out in enumerate((g0, g1, g2, g3)):
        out[...] = value[k * rows : (k + 1) * rows, :].astype(out.dtype)


def image_sum_kernel(g0, x1, x3, x2, image_grads):
    f32 = jnp.float32
    image_grads[...] = g0[...] + x1[...].astype(f32) + x2[...].astype(f32) + x3[...].astype(f32)


def text_sum_kernel(own, parts, text_grads, held, sems):
    y = lax.axis_index("yh")
    part = own.shape[0] // chunks
    moves = []
    for c in range(chunks):
        span = pl.ds(c * part, part)
        total = own[span, :]
        for step in range(1, sides):
            total = total + parts[lax.rem(y + step, sides), span, :].astype(jnp.float32)
        held[span, :] = total
        moves.append(pltpu.make_async_copy(held.at[span], text_grads.at[span], sems.at[c]))
        moves[-1].start()
    for move in moves:
        move.wait()


def call(kernel, shapes, scratch=(), flops=0, inputs=vmem, outputs=None, grant=48):
    def run(*operands):
        return pl.pallas_call(
            kernel,
            out_shape=shapes,
            in_specs=[inputs] * len(operands),
            out_specs=[vmem] * len(shapes) if outputs is None else outputs,
            scratch_shapes=list(scratch),
            compiler_params=pltpu.CompilerParams(vmem_limit_bytes=grant * 1024 * 1024),
            cost_estimate=pl.CostEstimate(flops=flops, bytes_accessed=4 << 20, transcendentals=0),
        )(*operands)

    return run


def on_device(image_embeddings, text_embeddings, pair_labels):
    rows, width = text_embeddings.shape
    scale = logit_scale / (sides * sides)
    f32 = jnp.float32
    block = (rows, width)
    every = sides * rows

    dots = 2 * rows * every * width
    half = jnp.bfloat16
    shape = jax.ShapeDtypeStruct

    (copies,) = call(
        copies_kernel,
        [shape((sides,) + block, half)],
        [pltpu.VMEM(block, half), pltpu.SemaphoreType.DMA((chunks,)), pltpu.SemaphoreType.DMA((chunks, sides))],
        inputs=hbm,
        outputs=[hbm],
        grant=60,
    )(text_embeddings)
    (bundle,) = call(bundle_kernel, [shape((rows + pad_rows, width), half)])(
        image_embeddings, pair_labels.reshape(1, rows)
    )
    stack = lax.all_to_all(copies, "yh", 0, 0)
    image_1 = shifted(bundle, "xx", 1)
    image_2 = shifted(bundle, "xx", 2)
    image_3 = shifted(bundle, "xx", -1)

    own, images, labels = call(
        functools.partial(near_kernel, scale),
        [shape(block, f32), shape((every, width), half), shape((1, every), f32)],
        [pltpu.VMEM((8, rows), f32)],
        2 * dots,
    )(bundle, image_1, image_2, image_3, text_embeddings)
    (parts,) = call(
        functools.partial(far_kernel, scale),
        [shape((sides,) + block, send_type)],
        [pltpu.VMEM(((sides - 1) * rows, width), half), pltpu.VMEM((sides - 1,) + block, send_type), pltpu.SemaphoreType.DMA((sides - 1,))],
        6 * dots,
        outputs=[hbm],
    )(stack, images, labels)
    parts = lax.all_to_all(parts, "yh", 0, 0)
    g0, g1, g2, g3 = call(
        functools.partial(image_kernel, scale),
        [shape(block, f32)] + [shape(block, send_type)] * 3,
        (),
        4 * dots,
    )(images, labels, stack)
    grad_1 = shifted(g1, "xx", -1)
    grad_2 = shifted(g2, "xx", 2)
    grad_3 = shifted(g3, "xx", 1)
    (image_grads,) = call(image_sum_kernel, [shape(block, f32)])(g0, grad_1, grad_3, grad_2)
    (text_grads,) = call(
        text_sum_kernel,
        [shape(block, f32)],
        [pltpu.VMEM(block, f32), pltpu.SemaphoreType.DMA((chunks,))],
        outputs=[hbm],
    )(own, parts)
    return image_grads, text_grads


def solution(mesh):
    grid = Mesh(mesh.devices.reshape(sides, sides, -1), ("yh", "xx", "dp"))
    rows = P(("dp", "yh", "xx"), None)
    return jax.shard_map(
        on_device,
        mesh=grid,
        in_specs=(rows, rows, P(("dp", "yh", "xx"))),
        out_specs=(rows, rows),
        check_vma=False,
    )
```
